128 devices in a mesh: gx: 4 (over z), gy: 8 (over y, core), gz: 4 (over x).
Axes of the slice: x: 4, y: 4, z: 4, core: 2. Of those that a mesh axis runs over, the one named last changes fastest.
Arguments:
- density: float32 [256, 2048, 1024], P('gz', 'gy', 'gx'), may hold values from 0 to 1
- depth_rank: int32 [4], replicated, may hold values from 0 to 15, as said below
- knots: int32 [8], replicated, may hold values from 0 to 255, as said below
- tf_color: float32 [3, 8], replicated, may hold values from 0.1 to 1
- tf_sigma: float32 [8], replicated, may hold values from 0.25 to 6
Outputs:
- image: float32 [8, 2048, 1024], P(None, ('gy', 'gz'), 'gx')
The draws below stay inside these ranges and needn't reach their ends.
Inputs may be any that keep to these rules, and one draw needn't show every extreme that they name: `depth_rank`: strictly increasing or strictly decreasing along the slabs, the ends being 0 and 15. `knots`: strictly increasing, the first 0 and the last 255.
All inputs are finite; a program needn't handle non-finite values.
Results may differ from the reference program's by a relative error of at most 0.0003.
Values sent between devices are 32-bit elements; how exact they have to be, the bound alone decides.
No kernel may reach another device: no remote copies, remote signals or barrier semaphores. Data moves between devices by JAX's collectives and lax.ppermute only.
A program may use at most 128 MiB of HBM per device.

```python
import math
import jax
import jax.numpy as jnp
from jax import lax

BINS = 256
CTRL = 8
NX = 1024
NY = 2048
NZ = 256
DEPTHS = 4


def draw_depth_rank(key, part):
    key = jax.random.fold_in(key, 11)
    key_flip, key_inner = jax.random.split(key)
    flipped = jax.random.randint(key_flip, (), 0, 2)
    top = 4 * DEPTHS - 1
    inner = jnp.sort(jax.random.permutation(key_inner, top - 1)[:DEPTHS - 2] + 1).astype(jnp.int32)
    ranks = jnp.concatenate([jnp.zeros((1,), jnp.int32), inner, jnp.full((1,), top, jnp.int32)])
    return jnp.where(flipped == 0, ranks, ranks[::-1]).astype(jnp.int32)


def draw_knots(key, part):
    key = jax.random.fold_in(key, 13)
    inner = jax.random.permutation(key, BINS - 2)[:CTRL - 2] + 1
    inner = jnp.sort(inner)
    first = jnp.zeros((1,), jnp.int32)
    final = jnp.full((1,), BINS - 1, jnp.int32)
    return jnp.concatenate([first, inner.astype(jnp.int32), final]).astype(jnp.int32)


def level_of(key, dims, cuts, least, largest):
    loudness = 1.0
    for dim, parts in cuts:
        steps = jax.random.uniform(jax.random.fold_in(jax.random.fold_in(key, 6), dim), (parts,), jnp.float32, least / len(cuts), largest / len(cuts))
        loudness = loudness * jnp.repeat(jnp.exp(steps), dims[dim] // parts).reshape((-1,) + (1,) * (len(dims) - 1 - dim))
    return loudness


def setup_inputs(seed: int = 0) -> dict:
    key_of = jax.random.split(jax.random.key(seed), 6)
    density = jnp.clip(1.0 * jax.random.uniform(key_of[0], (NZ, NY, NX), jnp.float32) ** level_of(key_of[0], (NZ, NY, NX), ((0, 4), (1, 8), (2, 4)), -0.2, 0.2), 0.0, 1.0)
    depth_rank = draw_depth_rank(jax.random.fold_in(key_of[5], 71), 0)
    knots = draw_knots(jax.random.fold_in(key_of[5], 71), 0)
    tf_color = jnp.clip(jax.random.uniform(key_of[3], (3, CTRL), jnp.float32, 0.1, 1.0), 0.1, 1.0)
    tf_sigma = jnp.clip(jnp.exp(jax.random.uniform(key_of[4], (CTRL,), jnp.float32, math.log(0.25), math.log(6.0))), 0.25, 6.0)
    return {"density": density, "depth_rank": depth_rank, "knots": knots, "tf_color": tf_color, "tf_sigma": tf_sigma}


def transfer(position, knots, tf_color, tf_sigma):
    knot_pos = knots.astype(jnp.float32)
    earlier = jnp.concatenate([knot_pos[:1] - 1.0, knot_pos[:-1]])
    later = jnp.concatenate([knot_pos[1:], knot_pos[-1:] + 1.0])
    sigma = jnp.zeros_like(position)
    red = jnp.zeros_like(position)
    green = jnp.zeros_like(position)
    blue = jnp.zeros_like(position)
    for index in range(knots.shape[0]):
        rising = jnp.clip((position - earlier[index]) / (knot_pos[index] - earlier[index]), 0.0, 1.0)
        falling = jnp.clip((later[index] - position) / (later[index] - knot_pos[index]), 0.0, 1.0)
        hat_value = jnp.minimum(rising, falling)
        sigma = sigma + hat_value * tf_sigma[index]
        red = red + hat_value * tf_color[0, index]
        green = green + hat_value * tf_color[1, index]
        blue = blue + hat_value * tf_color[2, index]
    return (sigma, red, green, blue)

def samples(slab, knots, tf_color, tf_sigma, inv_depth):
    center = slab[1:-1, 1:-1, 1:-1]
    grad_x = slab[1:-1, 1:-1, 2:] - slab[1:-1, 1:-1, :-2]
    grad_y = slab[1:-1, 2:, 1:-1] - slab[1:-1, :-2, 1:-1]
    grad_z = slab[2:, 1:-1, 1:-1] - slab[:-2, 1:-1, 1:-1]
    length = jnp.sqrt(grad_x * grad_x + grad_y * grad_y + grad_z * grad_z)
    factor = 1.0 / jnp.maximum(length, 0.5)
    normal_x = grad_x * factor
    normal_y = grad_y * factor
    normal_z = grad_z * factor
    shade = 0.3 + 0.7 * jnp.abs(0.48 * normal_x + 0.6 * normal_y + 0.64 * normal_z)
    sigma, red, green, blue = transfer(center * (BINS - 1.0), knots, tf_color, tf_sigma)
    tau = sigma * inv_depth
    return (tau, (red * shade, green * shade, blue * shade, normal_x, normal_y, normal_z))

def reference(density, depth_rank, knots, tf_color, tf_sigma):
    depth_count, rows_all, cols_all = density.shape
    inv_depth = 1.0 / depth_count
    forward = depth_rank[0] < depth_rank[depth_rank.shape[0] - 1]
    row_block = 8
    zpos = (jnp.arange(depth_count, dtype=jnp.float32) + 0.5) * inv_depth
    depth = jnp.where(forward, zpos, 1.0 - zpos)[:, None, None]
    zero_index = jnp.zeros((), jnp.int32)

    def one_block(start):
        start = start.astype(jnp.int32)
        main = lax.dynamic_slice(density, (zero_index, start, zero_index), (depth_count, row_block, cols_all))
        upper = jnp.maximum(start - 1, 0).astype(jnp.int32)
        above = lax.dynamic_slice(density, (zero_index, upper, zero_index), (depth_count, 1, cols_all))
        above = above * (start > 0).astype(density.dtype)
        lower = jnp.minimum(start + row_block, rows_all - 1).astype(jnp.int32)
        below = lax.dynamic_slice(density, (zero_index, lower, zero_index), (depth_count, 1, cols_all))
        below = below * (start + row_block < rows_all).astype(density.dtype)
        rows = jnp.concatenate([above, main, below], axis=1)
        slab = jnp.pad(rows, ((1, 1), (0, 0), (1, 1)))
        tau, feats = samples(slab, knots, tf_color, tf_sigma, inv_depth)
        running = jnp.cumsum(tau, axis=0)
        whole = running[-1]
        before = jnp.where(forward, running - tau, whole - running)
        weight = jnp.exp(-before) * (1.0 - jnp.exp(-tau))
        chans = [feats[0], feats[1], feats[2], None, depth, feats[3], feats[4], feats[5]]
        result = []
        for entry in chans:
            if entry is None:
                result.append(lax.optimization_barrier(jnp.sum(weight, axis=0)))
            else:
                result.append(lax.optimization_barrier(jnp.sum(weight * entry, axis=0)))
        return jnp.stack(result)
    starts = jnp.arange(rows_all // row_block, dtype=jnp.int32) * row_block
    blocks = lax.map(one_block, starts)
    return jnp.transpose(blocks, (1, 0, 2, 3)).reshape(8, rows_all, cols_all)
```

```python
import jax
import jax.numpy as jnp
from jax import lax
from jax.experimental import pallas as pl
from jax.experimental.pallas import tpu as pltpu
from jax.sharding import PartitionSpec as P

BINS = 256
LOG2E = 1.4426950408889634
KAPPA = 0.7 / 0.3
UNROLL = 16
ANY = pl.BlockSpec(memory_space=pl.ANY)
VMEM = pl.BlockSpec(memory_space=pltpu.VMEM)
SMEM = pl.BlockSpec(memory_space=pltpu.SMEM)


def neighbour(array, axis, step):
    size = lax.axis_size(axis)
    pairs = [(i, i + step) for i in range(size) if 0 <= i + step < size]
    return lax.ppermute(array, axis, pairs)


def shifted(array, axis, step):
    size = lax.axis_size(axis)
    return lax.ppermute(array, axis, [(i, (i + step) % size) for i in range(size)])


def columns_kernel(top_ref, bottom_ref, first_ref, last_ref):
    depth = top_ref.shape[0]
    lane = lax.broadcasted_iota(jnp.int32, (8, 128), 1)
    left_half = lane < 64

    def tile(index, _):
        rows = pl.ds(pl.multiple_of(index * 8, 8), 8)
        first = jnp.zeros((8, 128), jnp.float32)
        last = jnp.zeros((8, 128), jnp.float32)
        for half, ref in enumerate((top_ref, bottom_ref)):
            for z in range(depth):
                place = half * 64 + z
                ends = jnp.where(left_half, ref[z, rows, 0:128], ref[z, rows, 128:256])
                moved = ends if place == 0 else pltpu.roll(ends, place, 1)
                first = jnp.where(lane == place, moved, first)
                last = jnp.where(lane == (place - 1) % 128, moved, last)
        first_ref[rows, :] = first
        last_ref[rows, :] = pltpu.roll(last, 1, 1)
        return 0

    lax.fori_loop(0, first_ref.shape[0] // 8, tile, 0)


def columns(density):
    depth, rows, cols = density.shape
    half, block = rows // 2, 16
    steps = half // block
    return pl.pallas_call(
        columns_kernel,
        name="columns",
        grid=(steps,),
        out_shape=[jax.ShapeDtypeStruct((half, 128), jnp.float32)] * 2,
        in_specs=[
            pl.BlockSpec((depth, block, cols), lambda i: (0, i, 0)),
            pl.BlockSpec((depth, block, cols), lambda i: (0, i + steps, 0)),
        ],
        out_specs=[pl.BlockSpec((block, 128), lambda i: (i, 0))] * 2,
        compiler_params=pltpu.CompilerParams(vmem_limit_bytes=16 * 2**20),
        cost_estimate=pl.CostEstimate(flops=10**7, bytes_accessed=density.size * 4, transcendentals=0),
    )(density, density)


def march_kernel(
    shift, groups, rank_ref, knots_ref, color_ref, sigma_ref, x_hbm, zlo_hbm, zhi_hbm, ylo_ref, yhi_ref,
    xlo_hbm, xhi_hbm, out_ref, buf, lo_buf, hi_buf, sems, side_sems,
):
    depth, total_rows, _ = x_hbm.shape
    rows = out_ref.shape[1]
    tiles = rows // 8
    half = total_rows // 2
    mine = lax.axis_index("gz")
    piece = lax.rem(mine + shift, groups)
    y0 = pl.multiple_of(piece * rows, rows)
    forward = rank_ref[0] < rank_ref[groups - 1]
    is_first = piece == 0
    is_last = piece == groups - 1
    inv_depth = 1.0 / (depth * groups)

    def chunk(t, c):
        return pltpu.make_async_copy(
            x_hbm.at[:, pl.ds(pl.multiple_of(y0 + 8 * t, 8), 8), pl.ds(128 * c, 128)],
            buf.at[c, pl.ds(1, depth), pl.ds(pl.multiple_of(8 * (t + 1), 8), 8), :],
            sems.at[t + 1, c],
        )

    def face(c, end):
        return pltpu.make_async_copy(
            (zhi_hbm if end else zlo_hbm).at[pl.ds(y0, rows), pl.ds(128 * c, 128)],
            buf.at[c, (depth + 1) * end, pl.ds(8, rows), :],
            side_sems.at[end, c],
        )

    fold = pl.multiple_of(lax.rem(y0, half), rows)
    folded = jnp.where(y0 >= half, 64, 0)
    sides = [
        pltpu.make_async_copy(xlo_hbm.at[pl.ds(fold, rows), :], lo_buf, side_sems.at[2, 0]),
        pltpu.make_async_copy(xhi_hbm.at[pl.ds(fold, rows), :], hi_buf, side_sems.at[2, 1]),
    ] + [face(c, end) for c in range(2) for end in range(2)]
    for copy in sides:
        copy.start()

    @pl.when(jnp.logical_not(is_first))
    def _():
        for c in range(2):
            chunk(-1, c).start()

    for t in range(tiles):
        for c in range(2):
            chunk(t, c).start()

    @pl.when(jnp.logical_not(is_last))
    def _():
        for c in range(2):
            chunk(tiles, c).start()

    def put_row(ref, row):
        def body(group, _):
            for c in range(2):
                value = ref[pl.ds(pl.multiple_of(group * 8, 8), 8), pl.ds(128 * c, 128)]
                for k in range(8):
                    buf[c, 1 + group * 8 + k, pl.ds(row, 1), :] = value[k : k + 1, :]
            return 0

        lax.fori_loop(0, depth // 8, body, 0)

    @pl.when(is_first)
    def _():
        put_row(ylo_ref, 7)

    @pl.when(is_last)
    def _():
        put_row(yhi_ref, 8 + rows)

    def full(value):
        return jnp.full((8, 128), value, jnp.float32)

    knot = [knots_ref[k].astype(jnp.float32) * (1.0 / (BINS - 1.0)) for k in range(8)]
    widths = [full(knot[k + 1] - knot[k]) for k in range(7)]
    inverse = [1.0 / width for width in widths]
    scale = -LOG2E * inv_depth
    slopes = [full((sigma_ref[k + 1] - sigma_ref[k]) * scale) * inverse[k] for k in range(7)]
    base = full(sigma_ref[0] * scale)
    sign = jnp.where(forward, 1.0, -1.0)
    light_z = full(sign * (0.64 * KAPPA))
    offset = jnp.where(forward, mine, groups - 1 - mine) * depth
    depth_0 = (offset.astype(jnp.float32) + 0.5) * inv_depth
    step = jnp.where(forward, 1, -1)
    start = jnp.where(forward, 1, depth)
    lane = lax.broadcasted_iota(jnp.int32, (8, 128), 1)
    at_first = lane == 0
    at_last = lane == 127

    for copy in sides:
        copy.wait()

    @pl.when(jnp.logical_not(is_first))
    def _():
        for c in range(2):
            chunk(-1, c).wait()

    for c in range(2):
        chunk(0, c).wait()

    def tile(t, _):
        @pl.when(jnp.logical_or(t < tiles - 1, jnp.logical_not(is_last)))
        def _():
            for c in range(2):
                chunk(t + 1, c).wait()

        r = pl.multiple_of(8 * t + 8, 8)
        out_rows = pl.ds(pl.multiple_of(8 * t, 8), 8)
        side_lo = lo_buf[out_rows, :]
        side_hi = hi_buf[out_rows, :]
        zero = full(0.0)
        state = ((full(1.0),) + (zero,) * 12,) * 2
        before = tuple(buf[c, start - step, pl.ds(r, 8), :] for c in range(2))
        here = tuple(buf[c, start, pl.ds(r, 8), :] for c in range(2))

        def gradient_x(left, right, z):
            place = z - 1 + folded
            lo = pltpu.roll(side_lo, 128 - place, 1)
            hi = pltpu.roll(side_hi, 127 - place, 1)
            left_next, left_prev = pltpu.roll(left, 127, 1), pltpu.roll(left, 1, 1)
            right_next, right_prev = pltpu.roll(right, 127, 1), pltpu.roll(right, 1, 1)
            return (
                jnp.where(at_last, right_next, left_next) - jnp.where(at_first, lo, left_prev),
                jnp.where(at_last, hi, right_next) - jnp.where(at_first, left_prev, right_prev),
            )

        def block(b, carry):
            before, here, state = carry
            state = [list(s) for s in state]
            for k in range(UNROLL):
                z = start + step * (b * UNROLL + k)
                after = tuple(buf[c, z + step, pl.ds(r, 8), :] for c in range(2))
                grad_x = gradient_x(here[0], here[1], z)
                for c in range(2):
                    s = state[c]
                    gx = grad_x[c]
                    gy = buf[c, z, pl.ds(r + 1, 8), :] - buf[c, z, pl.ds(r - 1, 8), :]
                    gz = after[c] - before[c]
                    factor = lax.rsqrt(jnp.maximum(gx * gx + gy * gy + gz * gz, 0.25))
                    light = gx * (0.48 * KAPPA) + gy * (0.6 * KAPPA) + gz * light_z
                    rest = here[c]
                    ramps = []
                    power = base
                    for j in range(7):
                        ramp = jnp.minimum(rest, widths[j]) if j < 6 else rest
                        rest = rest - ramp
                        ramps.append(ramp)
                        power = power + ramp * slopes[j]
                    clear = s[0] * jnp.exp2(power)
                    weight = s[0] - clear
                    scaled = weight * factor
                    shaded = weight + scaled * jnp.abs(light)
                    s[1] = s[1] + s[0]
                    s[0] = clear
                    s[2] = s[2] + shaded
                    for j in range(7):
                        s[3 + j] = s[3 + j] + shaded * ramps[j]
                    s[10] = s[10] + scaled * gx
                    s[11] = s[11] + scaled * gy
                    s[12] = s[12] + scaled * gz
                before, here = here, after
            return before, here, tuple(tuple(s) for s in state)

        _, _, state = lax.fori_loop(0, depth // UNROLL, block, (before, here, state))
        for c in range(2):
            s = state[c]
            cols = pl.ds(128 * c, 128)
            for channel in range(3):
                total = s[2] * (color_ref[channel, 0] * 0.3)
                for j in range(7):
                    rise = (color_ref[channel, j + 1] - color_ref[channel, j]) * 0.3
                    total = total + s[3 + j] * (inverse[j] * rise)
                out_ref[channel, out_rows, cols] = total
            opacity = 1.0 - s[0]
            out_ref[3, out_rows, cols] = opacity
            out_ref[4, out_rows, cols] = opacity * depth_0 + (s[1] - 1.0 - s[0] * (depth - 1.0)) * inv_depth
            out_ref[5, out_rows, cols] = s[10]
            out_ref[6, out_rows, cols] = s[11]
            out_ref[7, out_rows, cols] = s[12] * sign
        return 0

    lax.fori_loop(0, tiles, tile, 0)


def march(shift, groups, tables, density, sides):
    depth, total_rows, cols = density.shape
    rows = total_rows // groups
    voxels = depth * rows * cols

    def kernel(*refs):
        march_kernel(shift, groups, *refs)

    return pl.pallas_call(
        kernel,
        name="march",
        out_shape=jax.ShapeDtypeStruct((8, rows, cols), jnp.float32),
        in_specs=[SMEM] * 4 + [ANY] * 3 + [VMEM] * 2 + [ANY] * 2,
        out_specs=VMEM,
        scratch_shapes=[
            pltpu.VMEM((2, depth + 2, rows + 16, 128), jnp.float32),
            pltpu.VMEM((rows, 128), jnp.float32),
            pltpu.VMEM((rows, 128), jnp.float32),
            pltpu.SemaphoreType.DMA((rows // 8 + 2, 2)),
            pltpu.SemaphoreType.DMA((3, 2)),
        ],
        compiler_params=pltpu.CompilerParams(vmem_limit_bytes=24 * 2**20),
        cost_estimate=pl.CostEstimate(flops=72 * voxels, bytes_accessed=voxels * 4, transcendentals=2 * voxels),
    )(*tables, density, *sides)


def body(density, depth_rank, knots, tf_color, tf_sigma):
    depth, rows, cols = density.shape
    groups = lax.axis_size("gz")
    zlo = neighbour(density[depth - 1], "gz", 1)
    zhi = neighbour(density[0], "gz", -1)
    ylo = neighbour(density[:, rows - 1, :], "gy", 1)
    yhi = neighbour(density[:, 0, :], "gy", -1)
    first, last = columns(density)
    xlo = neighbour(last, "gx", 1)
    xhi = neighbour(first, "gx", -1)
    tables = (depth_rank, knots, tf_color, tf_sigma)
    sides = (zlo, zhi, ylo, yhi, xlo, xhi)
    parts = [None] * groups
    for shift in (2, 1, 3, 0):
        piece = march(shift, groups, tables, density, sides)
        parts[shift] = piece if shift == 0 else shifted(piece, "gz", shift)
    mine = lax.axis_index("gz")
    forward = depth_rank[0] < depth_rank[groups - 1]
    slabs = [lax.rem(mine - s + groups, groups) for s in range(groups)]
    image = 0.0
    for s in range(groups):
        seen = parts[s]
        for other in range(groups):
            if other != s:
                nearer = (slabs[other] < slabs[s]) == forward
                seen = seen * jnp.where(nearer, 1.0 - parts[other][3:4], 1.0)
        image = image + seen
    return image


def solution(mesh):
    in_specs = (P("gz", "gy", "gx"), P(), P(), P(), P())
    out_specs = P(None, ("gy", "gz"), "gx")
    return jax.shard_map(body, mesh=mesh, in_specs=in_specs, out_specs=out_specs, check_vma=False)
```

```python
import jax
import jax.numpy as jnp
from jax import lax
from jax.experimental import pallas as pl
from jax.experimental.pallas import tpu as pltpu
from jax.sharding import PartitionSpec as P

BINS = 256
LOG2E = 1.4426950408889634
KAPPA = 0.7 / 0.3
UNROLL = 64
SPLIT = 4
AHEAD = 5
ROOM = 50 * 2**20
ANY = pl.BlockSpec(memory_space=pl.ANY)
VMEM = pl.BlockSpec(memory_space=pltpu.VMEM)
SMEM = pl.BlockSpec(memory_space=pltpu.SMEM)


def neighbour(array, axis, step):
    size = lax.axis_size(axis)
    pairs = [(i, i + step) for i in range(size) if 0 <= i + step < size]
    return lax.ppermute(array, axis, pairs)


def shifted(array, axis, step):
    size = lax.axis_size(axis)
    return lax.ppermute(array, axis, [(i, (i + step) % size) for i in range(size)])


def layers_kernel(x_hbm, x_first, x_last, y_first, y_last, z_first, z_last, buf, sems, z_sems):
    depth, rows, _ = x_hbm.shape
    tiles = rows // 8
    planes = [
        pltpu.make_async_copy(x_hbm.at[0], z_first, z_sems.at[0]),
        pltpu.make_async_copy(x_hbm.at[depth - 1], z_last, z_sems.at[1]),
    ]

    def chunk(t):
        at = pl.ds(pl.multiple_of(8 * t, 8), 8)
        return pltpu.make_async_copy(x_hbm.at[:, at, :], buf.at[:, at, :], sems.at[t])

    for t in range(tiles // 2):
        chunk(t).start()
        chunk(t + tiles // 2).start()
    for plane in planes:
        plane.start()
    lane = lax.broadcasted_iota(jnp.int32, (8, 128), 1)
    left_half = lane < 64

    def tile(t, _):
        first = jnp.zeros((8, 128), jnp.float32)
        last = jnp.zeros((8, 128), jnp.float32)
        for half in range(2):
            row_tile = t + half * (tiles // 2)
            chunk(row_tile).wait()
            at = pl.ds(pl.multiple_of(8 * row_tile, 8), 8)
            for z in range(depth):
                place = half * 64 + z
                ends = jnp.where(left_half, buf[z, at, 0:128], buf[z, at, 128:256])
                moved = ends if place == 0 else pltpu.roll(ends, place, 1)
                first = jnp.where(lane == place, moved, first)
                last = jnp.where(lane == (place - 1) % 128, moved, last)
        at = pl.ds(pl.multiple_of(8 * t, 8), 8)
        x_first[at, :] = first
        x_last[at, :] = pltpu.roll(last, 1, 1)
        return 0

    lax.fori_loop(0, tiles // 2, tile, 0)
    for z in range(depth):
        y_first[pl.ds(z, 1), :] = buf[z, pl.ds(0, 1), :]
        y_last[pl.ds(z, 1), :] = buf[z, pl.ds(rows - 1, 1), :]
    for plane in planes:
        plane.wait()


def layers(density):
    depth, rows, cols = density.shape
    shape = lambda *dims: jax.ShapeDtypeStruct(dims, jnp.float32)
    return pl.pallas_call(
        layers_kernel,
        name="layers",
        out_shape=[shape(rows // 2, 128)] * 2 + [shape(depth, cols)] * 2 + [shape(rows, cols)] * 2,
        in_specs=[ANY],
        out_specs=[VMEM] * 4 + [ANY] * 2,
        scratch_shapes=[
            pltpu.VMEM(density.shape, jnp.float32),
            pltpu.SemaphoreType.DMA((rows // 8,)),
            pltpu.SemaphoreType.DMA((2,)),
        ],
        compiler_params=pltpu.CompilerParams(vmem_limit_bytes=ROOM),
        cost_estimate=pl.CostEstimate(flops=10**7, bytes_accessed=density.size * 4, transcendentals=0),
    )(density)


def march_kernel(
    shift, groups, rank_ref, knots_ref, color_ref, sigma_ref, x_hbm, zlo_hbm, zhi_hbm, ylo_ref, yhi_ref,
    xlo_hbm, xhi_hbm, out_ref, buf, lo_buf, hi_buf, sems, side_sems,
):
    depth, total_rows, _ = x_hbm.shape
    rows = out_ref.shape[1]
    tiles = rows // 8
    half = total_rows // 2
    mine = lax.axis_index("gz")
    piece = lax.rem(mine + shift, groups)
    y0 = pl.multiple_of(piece * rows, rows)
    forward = rank_ref[0] < rank_ref[groups - 1]
    is_first = piece == 0
    is_last = piece == groups - 1
    inv_depth = 1.0 / (depth * groups)

    def chunk(t, c):
        return pltpu.make_async_copy(
            x_hbm.at[:, pl.ds(pl.multiple_of(y0 + 8 * t, 8), 8), pl.ds(128 * c, 128)],
            buf.at[c, pl.ds(1, depth), pl.ds(pl.multiple_of(8 * (t + 1), 8), 8), :],
            sems.at[t + 1, c],
        )

    def face(c, end):
        return pltpu.make_async_copy(
            (zhi_hbm if end else zlo_hbm).at[pl.ds(y0, rows), pl.ds(128 * c, 128)],
            buf.at[c, (depth + 1) * end, pl.ds(8, rows), :],
            side_sems.at[end, c],
        )

    fold = pl.multiple_of(lax.rem(y0, half), rows)
    folded = jnp.where(y0 >= half, 64, 0)
    sides = [
        pltpu.make_async_copy(xlo_hbm.at[pl.ds(fold, rows), :], lo_buf, side_sems.at[2, 0]),
        pltpu.make_async_copy(xhi_hbm.at[pl.ds(fold, rows), :], hi_buf, side_sems.at[2, 1]),
    ] + [face(c, end) for c in range(2) for end in range(2)]
    for copy in sides:
        copy.start()

    def begin(t, parts):
        each = depth // parts
        for k in range(parts):
            for c in range(2):
                pltpu.make_async_copy(
                    x_hbm.at[pl.ds(k * each, each), pl.ds(pl.multiple_of(y0 + 8 * t, 8), 8), pl.ds(128 * c, 128)],
                    buf.at[c, pl.ds(1 + k * each, each), pl.ds(pl.multiple_of(8 * (t + 1), 8), 8), :],
                    sems.at[t + 1, c],
                ).start()

    @pl.when(jnp.logical_not(is_first))
    def _():
        begin(-1, SPLIT)

    for t in range(AHEAD):
        begin(t, SPLIT if t < 2 else 1)

    def put_row(ref, row):
        def body(group, _):
            for c in range(2):
                value = ref[pl.ds(pl.multiple_of(group * 8, 8), 8), pl.ds(128 * c, 128)]
                for k in range(8):
                    buf[c, 1 + group * 8 + k, pl.ds(row, 1), :] = value[k : k + 1, :]
            return 0

        lax.fori_loop(0, depth // 8, body, 0)

    @pl.when(is_first)
    def _():
        put_row(ylo_ref, 7)

    @pl.when(is_last)
    def _():
        put_row(yhi_ref, 8 + rows)

    def full(value):
        return jnp.full((8, 128), value, jnp.float32)

    knot = [knots_ref[k].astype(jnp.float32) * (1.0 / (BINS - 1.0)) for k in range(8)]
    widths = [full(knot[k + 1] - knot[k]) for k in range(7)]
    inverse = [1.0 / width for width in widths]
    scale = -LOG2E * inv_depth
    slopes = [full((sigma_ref[k + 1] - sigma_ref[k]) * scale) * inverse[k] for k in range(7)]
    base = full(sigma_ref[0] * scale)
    sign = jnp.where(forward, 1.0, -1.0)
    light_z = full(sign * (0.64 * KAPPA))
    offset = jnp.where(forward, mine, groups - 1 - mine) * depth
    depth_0 = (offset.astype(jnp.float32) + 0.5) * inv_depth
    step = jnp.where(forward, 1, -1)
    start = jnp.where(forward, 1, depth)
    lane = lax.broadcasted_iota(jnp.int32, (8, 128), 1)
    at_first = lane == 0
    at_last = lane == 127

    for copy in sides:
        copy.wait()

    @pl.when(jnp.logical_not(is_first))
    def _():
        for c in range(2):
            chunk(-1, c).wait()

    for c in range(2):
        chunk(0, c).wait()

    def tile(t, _):
        @pl.when(jnp.logical_or(t < tiles - 1, jnp.logical_not(is_last)))
        def _():
            for c in range(2):
                chunk(t + 1, c).wait()

        @pl.when(jnp.logical_or(t < tiles - AHEAD, jnp.logical_and(t == tiles - AHEAD, jnp.logical_not(is_last))))
        def _():
            begin(t + AHEAD, 1)

        r = pl.multiple_of(8 * t + 8, 8)
        out_rows = pl.ds(pl.multiple_of(8 * t, 8), 8)
        side_lo = lo_buf[out_rows, :]
        side_hi = hi_buf[out_rows, :]
        zero = full(0.0)
        state = ((full(1.0),) + (zero,) * 12,) * 2
        before = tuple(buf[c, start - step, pl.ds(r, 8), :] for c in range(2))
        here = tuple(buf[c, start, pl.ds(r, 8), :] for c in range(2))

        def gradient_x(left, right, z):
            place = z - 1 + folded
            lo = pltpu.roll(side_lo, 128 - place, 1)
            hi = pltpu.roll(side_hi, 127 - place, 1)
            left_next, left_prev = pltpu.roll(left, 127, 1), pltpu.roll(left, 1, 1)
            right_next, right_prev = pltpu.roll(right, 127, 1), pltpu.roll(right, 1, 1)
            return (
                jnp.where(at_last, right_next, left_next) - jnp.where(at_first, lo, left_prev),
                jnp.where(at_last, hi, right_next) - jnp.where(at_first, left_prev, right_prev),
            )

        def block(b, carry):
            before, here, state = carry
            state = [list(s) for s in state]
            for k in range(UNROLL):
                z = start + step * (b * UNROLL + k)
                after = tuple(buf[c, z + step, pl.ds(r, 8), :] for c in range(2))
                grad_x = gradient_x(here[0], here[1], z)
                for c in range(2):
                    s = state[c]
                    gx = grad_x[c]
                    gy = buf[c, z, pl.ds(r + 1, 8), :] - buf[c, z, pl.ds(r - 1, 8), :]
                    gz = after[c] - before[c]
                    factor = lax.rsqrt(jnp.maximum(gx * gx + gy * gy + gz * gz, 0.25))
                    light = gx * (0.48 * KAPPA) + gy * (0.6 * KAPPA) + gz * light_z
                    rest = here[c]
                    ramps = []
                    power = base
                    for j in range(7):
                        ramp = jnp.minimum(rest, widths[j]) if j < 6 else rest
                        rest = rest - ramp
                        ramps.append(ramp)
                        power = power + ramp * slopes[j]
                    clear = s[0] * jnp.exp2(power)
                    weight = s[0] - clear
                    scaled = weight * factor
                    shaded = weight + scaled * jnp.abs(light)
                    s[1] = s[1] + s[0]
                    s[0] = clear
                    s[2] = s[2] + shaded
                    for j in range(7):
                        s[3 + j] = s[3 + j] + shaded * ramps[j]
                    s[10] = s[10] + scaled * gx
                    s[11] = s[11] + scaled * gy
                    s[12] = s[12] + scaled * gz
                before, here = here, after
            return before, here, tuple(tuple(s) for s in state)

        _, _, state = lax.fori_loop(0, depth // UNROLL, block, (before, here, state))
        for c in range(2):
            s = state[c]
            cols = pl.ds(128 * c, 128)
            for channel in range(3):
                total = s[2] * (color_ref[channel, 0] * 0.3)
                for j in range(7):
                    rise = (color_ref[channel, j + 1] - color_ref[channel, j]) * 0.3
                    total = total + s[3 + j] * (inverse[j] * rise)
                out_ref[channel, out_rows, cols] = total
            opacity = 1.0 - s[0]
            out_ref[3, out_rows, cols] = opacity
            out_ref[4, out_rows, cols] = opacity * depth_0 + (s[1] - 1.0 - s[0] * (depth - 1.0)) * inv_depth
            out_ref[5, out_rows, cols] = s[10]
            out_ref[6, out_rows, cols] = s[11]
            out_ref[7, out_rows, cols] = s[12] * sign
        return 0

    lax.fori_loop(0, tiles, tile, 0)


def march(shift, groups, tables, density, sides):
    depth, total_rows, cols = density.shape
    rows = total_rows // groups
    voxels = depth * rows * cols

    def kernel(*refs):
        march_kernel(shift, groups, *refs)

    return pl.pallas_call(
        kernel,
        name="march",
        out_shape=jax.ShapeDtypeStruct((8, rows, cols), jnp.float32),
        in_specs=[SMEM] * 4 + [ANY] * 3 + [VMEM] * 2 + [ANY] * 2,
        out_specs=VMEM,
        scratch_shapes=[
            pltpu.VMEM((2, depth + 2, rows + 16, 128), jnp.float32),
            pltpu.VMEM((rows, 128), jnp.float32),
            pltpu.VMEM((rows, 128), jnp.float32),
            pltpu.SemaphoreType.DMA((rows // 8 + 2, 2)),
            pltpu.SemaphoreType.DMA((3, 2)),
        ],
        compiler_params=pltpu.CompilerParams(vmem_limit_bytes=ROOM),
        cost_estimate=pl.CostEstimate(flops=72 * voxels, bytes_accessed=voxels * 4, transcendentals=2 * voxels),
    )(*tables, density, *sides)


def compose_kernel(groups, rank_ref, *refs):
    parts, out_ref = refs[:groups], refs[groups]
    mine = lax.axis_index("gz")
    forward = rank_ref[0] < rank_ref[groups - 1]
    place = []
    for s in range(groups):
        slab = lax.rem(mine - s + groups, groups)
        place.append(jnp.where(forward, slab, groups - 1 - slab))
    nearer = [[jnp.where(place[o] < place[s], 1.0, 0.0) for o in range(groups)] for s in range(groups)]

    def tile(t, _):
        at = pl.ds(pl.multiple_of(8 * t, 8), 8)
        opacity = [part[3, at, :] for part in parts]
        dims = []
        for s in range(groups):
            dim = 1.0
            for o in range(groups):
                if o != s:
                    dim = dim * (1.0 - opacity[o] * nearer[s][o])
            dims.append(dim)
        for channel in range(8):
            total = dims[0] * parts[0][channel, at, :]
            for s in range(1, groups):
                total = total + dims[s] * parts[s][channel, at, :]
            out_ref[channel, at, :] = total
        return 0

    lax.fori_loop(0, out_ref.shape[1] // 8, tile, 0)


def compose(rank, parts):
    groups = len(parts)

    def kernel(*refs):
        compose_kernel(groups, *refs)

    return pl.pallas_call(
        kernel,
        name="compose",
        out_shape=jax.ShapeDtypeStruct(parts[0].shape, jnp.float32),
        in_specs=[SMEM] + [VMEM] * groups,
        out_specs=VMEM,
        compiler_params=pltpu.CompilerParams(vmem_limit_bytes=32 * 2**20),
        cost_estimate=pl.CostEstimate(flops=10**6, bytes_accessed=5 * parts[0].size * 4, transcendentals=0),
    )(rank, *parts)


def body(density, depth_rank, knots, tf_color, tf_sigma):
    groups = lax.axis_size("gz")
    x_first, x_last, y_first, y_last, z_first, z_last = layers(density)
    zlo = neighbour(z_last, "gz", 1)
    zhi = neighbour(z_first, "gz", -1)
    xlo = neighbour(x_last, "gx", 1)
    xhi = neighbour(x_first, "gx", -1)
    ylo = neighbour(y_last, "gy", 1)
    yhi = neighbour(y_first, "gy", -1)
    tables = (depth_rank, knots, tf_color, tf_sigma)
    sides = (zlo, zhi, ylo, yhi, xlo, xhi)
    parts = [None] * groups
    for shift in (2, 1, 3, 0):
        piece = march(shift, groups, tables, density, sides)
        parts[shift] = piece if shift == 0 else shifted(piece, "gz", shift)
    return compose(depth_rank, parts)


def solution(mesh):
    in_specs = (P("gz", "gy", "gx"), P(), P(), P(), P())
    out_specs = P(None, ("gy", "gz"), "gx")
    return jax.shard_map(body, mesh=mesh, in_specs=in_specs, out_specs=out_specs, check_vma=False)
```
